32 devices in a mesh: region: 2 (over x), inner: 16 (over z, y, core).
Axes of the slice: x: 2, y: 2, z: 4, core: 2. Of those that a mesh axis runs over, the one named last changes fastest.
Arguments:
- density: float32 [6, 48, 144], P('region', 'inner'), may hold values from 0.8 to 1.2
- momentum: float32 [3, 6, 48, 144], P(None, 'region', 'inner'), may hold values from -1 to 1
- energy: float32 [6, 48, 144], P('region', 'inner'), may hold values from 4 to 5
- fuel_density: float32 [6, 48, 144], P('region', 'inner'), may hold values from 0.02 to 0.2
- drop_pos: float32 [3, 65536], P(None, ('region', 'inner')), may hold values from -1 to 1
- drop_vel: float32 [3, 65536], P(None, ('region', 'inner')), may hold values from -3 to 3
- drop_mass: float32 [65536], P(('region', 'inner')), may hold values from 0.5 to 2
- block_cell: int32 [2048], P(('region', 'inner')), may hold values from 0 to 767, as said below
- block_count: int32 [2048], P(('region', 'inner')), may hold values from 1 to 32, as said below
Outputs:
- gas_state: float32 [6, 6, 48, 144], P(None, 'region', 'inner')
- drop_vel_out: float32 [3, 65536], P(None, ('region', 'inner'))
- drop_mass_out: float32 [65536], P(('region', 'inner'))
The draws below stay inside these ranges and needn't reach their ends.
Inputs may be any that keep to these rules, and one draw needn't show every extreme that they name: `block_cell`: within the 64 blocks of one device the ids never fall. With owner = id // 48, at most 8 blocks of one device lie on the hexahedra of one owner; on every device some owner has exactly 8, and in every region one owner has exactly 8 from every device of the region. `block_count`: every device has a block with 32 live droplets.
All inputs are finite; a program needn't handle non-finite values.
Results may differ from the reference program's by a relative error of at most 0.00005.
Values sent between devices are 32-bit elements; how exact they have to be, the bound alone decides.
A program may use at most 64 MiB of HBM per device.

```python
import math
import jax
import jax.numpy as jnp
from jax import lax

EZ = 48
CAP = 8
PB = 32
NB = 64
RBLK = 1024
NDROP = 65536
NXN = 6
NYN = 48
NZN = 144
N_REGION = 2
N_INNER = 16


def draw_block_cell(key, part):
    key = jax.random.fold_in(key, 11)
    half_cap = CAP // 2
    per_device = N_INNER * half_cap
    devices = N_REGION * N_INNER
    score_key, shift_key, crowd_key, local_key = jax.random.split(key, 4)
    scores = jax.random.randint(score_key, (devices, N_INNER), 0, 1 << 20) * N_INNER + jnp.arange(N_INNER)[None, :]
    ordering = jnp.argsort(scores, axis=1).astype(jnp.int32)
    crowded = jax.random.randint(crowd_key, (N_REGION,), 0, N_INNER)
    crowded_dev = jnp.repeat(crowded, N_INNER)
    position = jnp.argmax((ordering == crowded_dev[:, None]).astype(jnp.int32), axis=1)
    leader = ordering[:, 0]
    column = jnp.arange(N_INNER)[None, :]
    ordering = jnp.where(column == 0, crowded_dev[:, None], jnp.where(column == position[:, None], leader[:, None], ordering))
    shifts = jax.random.randint(shift_key, (devices, N_INNER // 2), -half_cap, half_cap + 1)
    shifts = shifts.at[:, 0].set(half_cap)
    loads_pair = jnp.stack([half_cap + shifts, half_cap - shifts], 2).reshape(devices, N_INNER)
    owner_loads = jnp.zeros((devices, N_INNER), jnp.int32).at[jnp.arange(devices)[:, None], ordering].set(loads_pair)
    bounds = jnp.cumsum(owner_loads, axis=1)
    owners = jnp.sum((bounds[:, None, :] <= jnp.arange(per_device)[None, :, None]).astype(jnp.int32), axis=2)
    local_cells = jax.random.randint(local_key, (devices, per_device), 0, EZ)
    cell_ids = jnp.sort(owners * EZ + local_cells, axis=1)
    return cell_ids.reshape(-1).astype(jnp.int32)


def draw_block_count(key, part):
    key = jax.random.fold_in(key, 23)
    per_device = N_INNER * (CAP // 2)
    devices = N_REGION * N_INNER
    count_key, spot_key = jax.random.split(key, 2)
    counts_drawn = jax.random.randint(count_key, (devices, per_device), 1, PB + 1)
    spot_index = jax.random.randint(spot_key, (devices, 1), 0, per_device)
    counts_drawn = jnp.where(jnp.arange(per_device)[None, :] == spot_index, PB, counts_drawn)
    return counts_drawn.reshape(-1).astype(jnp.int32)


def shard_levels(stream_key, dims, cuts, smallest, largest):
    def one(dim, shards_of):
        heights = jax.random.uniform(jax.random.fold_in(jax.random.fold_in(stream_key, 6), dim), (shards_of,), jnp.float32, smallest / len(cuts), largest / len(cuts))
        return jnp.repeat(jnp.exp(heights), dims[dim] // shards_of).reshape((-1,) + (1,) * (len(dims) - dim - 1))

    level = one(*cuts[0])
    for cut in cuts[1:]:
        level = level * one(*cut)
    return level


def scatter_about(key, dims, deviation, bound, pieces=(), dtype=jnp.bfloat16):
    values = jax.random.normal(key, dims, jnp.float32) * deviation
    if len(pieces) > 0:
        values = shard_levels(key, dims, pieces, -0.22, 0.18) * values
    return jnp.clip(values, min=-bound, max=bound).astype(dtype)


def setup_inputs(seed: int = 0) -> dict:
    splits = jax.random.split(jax.random.key(seed), 10)
    return {
        "density": jnp.clip(0.8 + 0.40000004 * jax.random.uniform(splits[0], (NXN, NYN, NZN), jnp.float32) ** shard_levels(splits[0], (NXN, NYN, NZN), ((0, 2), (1, 16)), -0.2, 0.2), 0.8, 1.2),
        "momentum": jnp.clip(jax.random.uniform(splits[1], (3, NXN, NYN, NZN), jnp.float32, -1.0, 1.0) * shard_levels(splits[1], (3, NXN, NYN, NZN), ((1, 2), (2, 16)), -0.4, 0.0), -1.0, 1.0),
        "energy": jnp.clip(4.0 + 1.0 * jax.random.uniform(splits[2], (NXN, NYN, NZN), jnp.float32) ** shard_levels(splits[2], (NXN, NYN, NZN), ((0, 2), (1, 16)), -0.2, 0.2), 4.0, 5.0),
        "fuel_density": jnp.clip(0.02 + 0.18 * jax.random.uniform(splits[3], (NXN, NYN, NZN), jnp.float32) ** shard_levels(splits[3], (NXN, NYN, NZN), ((0, 2), (1, 16)), -0.2, 0.2), 0.02, 0.2),
        "drop_pos": jnp.clip(jax.random.uniform(splits[4], (3, NDROP), jnp.float32, -1.0, 1.0) * shard_levels(splits[4], (3, NDROP), ((1, 32),), -0.4, 0.0), -1.0, 1.0),
        "drop_vel": scatter_about(splits[5], (3, NDROP), 0.3, 3.0, ((1, 32),), jnp.float32),
        "drop_mass": jnp.clip(jnp.exp(math.log(2.0) - 1.3862944 * jax.random.uniform(splits[6], (NDROP,), jnp.float32) ** shard_levels(splits[6], (NDROP,), ((0, 32),), -0.2, 0.2)), 0.5, 2.0),
        "block_cell": draw_block_cell(jax.random.fold_in(splits[9], 71), 0),
        "block_count": draw_block_count(jax.random.fold_in(splits[9], 71), 0),
    }


GAMMA = 1.4
TIME_STEP = 0.05
EVAP_RATE = 0.5
LATENT = 0.5
END_WEIGHT = 1.0 / 3.0

def derivative_matrix():
    return jnp.array([[-1.5, 2.0, -0.5], [-0.5, 0.0, 0.5], [0.5, -2.0, 1.5]], jnp.float32)

def node_weights():
    gll_line = jnp.array([1.0 / 3.0, 4.0 / 3.0, 1.0 / 3.0], jnp.float32)
    return (gll_line[:, None, None] * gll_line[None, :, None] * gll_line[None, None, :]).reshape(27)

def euler_flux(conserved, direction):
    pressure_node = (GAMMA - 1.0) * (conserved[4] - 0.5 * (conserved[1] ** 2 + conserved[2] ** 2 + conserved[3] ** 2) / conserved[0])
    normal_speed = conserved[1 + direction] / conserved[0]
    flux_rows = [conserved[1 + direction]]
    for component in range(3):
        momentum_flux = conserved[1 + component] * normal_speed
        if component == direction:
            momentum_flux = momentum_flux + pressure_node
        flux_rows.append(momentum_flux)
    flux_rows.append((conserved[4] + pressure_node) * normal_speed)
    flux_rows.append(conserved[5] * normal_speed)
    return (jnp.stack(flux_rows), normal_speed, pressure_node)

def face_flux(state_left, state_right, direction):
    flux_left, speed_left, pressure_left = euler_flux(state_left, direction)
    flux_right, speed_right, pressure_right = euler_flux(state_right, direction)
    wave_left = jnp.abs(speed_left) + jnp.sqrt(GAMMA * pressure_left / state_left[0])
    wave_right = jnp.abs(speed_right) + jnp.sqrt(GAMMA * pressure_right / state_right[0])
    wave_speed = jnp.maximum(wave_left, wave_right)
    return 0.5 * (flux_left + flux_right) - 0.5 * wave_speed * (state_right - state_left)

def axis_tendency(padded, along_axis, direction):
    shifted_axes = jnp.moveaxis(padded, along_axis, -1)
    length = shifted_axes.shape[-1] - 2
    elements = length // 3
    interior = shifted_axes[..., 1:-1]
    flux_nodes, unused_speed, unused_pressure = euler_flux(interior, direction)
    grouped = flux_nodes.reshape(flux_nodes.shape[:-1] + (elements, 3))
    volume = jnp.einsum('...j,ij->...i', grouped, derivative_matrix(), precision=lax.Precision.HIGHEST)
    outer_left = shifted_axes[..., 0:length + 1:3]
    outer_right = shifted_axes[..., 1:length + 2:3]
    face_values = face_flux(outer_left, outer_right, direction)
    lift_first = -(face_values[..., :-1] - grouped[..., 0]) / END_WEIGHT
    lift_last = (face_values[..., 1:] - grouped[..., 2]) / END_WEIGHT
    lifted = jnp.stack([lift_first, jnp.zeros_like(lift_first), lift_last], -1)
    result = -(volume + lifted)
    return jnp.moveaxis(result.reshape(result.shape[:-2] + (length,)), -1, along_axis)

def fluid_tendency(conserved):
    along_x = axis_tendency(jnp.pad(conserved, ((0, 0), (1, 1), (0, 0), (0, 0)), mode='wrap'), 1, 0)
    along_y = axis_tendency(jnp.pad(conserved, ((0, 0), (0, 0), (1, 1), (0, 0)), mode='wrap'), 2, 1)
    along_z = axis_tendency(jnp.pad(conserved, ((0, 0), (0, 0), (0, 0), (1, 1)), mode='wrap'), 3, 2)
    return along_x + along_y + along_z

def lagrange_weights(positions):
    basis_values = jnp.stack([0.5 * positions * (positions - 1.0), 1.0 - positions * positions, 0.5 * positions * (positions + 1.0)])
    weights = basis_values[:, None, None, 0] * basis_values[None, :, None, 1] * basis_values[None, None, :, 2]
    return weights.reshape((27,) + positions.shape[1:])

def droplet_terms(block_states, weights, velocity, droplet_mass, live_slots, parcel):
    gas_values = jnp.einsum('bfk,kbp->fbp', block_states, weights, precision=lax.Precision.HIGHEST)
    relative = gas_values[1:4] / gas_values[0] - velocity
    fuel_share = gas_values[5] / gas_values[0]
    cube_root = jnp.exp(jnp.log(droplet_mass) / 3.0)
    acceleration = live_slots * relative / (cube_root * cube_root)
    evaporation = live_slots * EVAP_RATE * cube_root * jnp.sqrt(1.0 + lax.optimization_barrier(jnp.sum(relative * relative, 0))) * (1.0 - fuel_share)
    drag_force = droplet_mass * acceleration
    sources = jnp.stack([evaporation, evaporation * velocity[0] - drag_force[0], evaporation * velocity[1] - drag_force[1], evaporation * velocity[2] - drag_force[2], evaporation * (LATENT + 0.5 * lax.optimization_barrier(jnp.sum(velocity * velocity, 0))) - lax.optimization_barrier(jnp.sum(drag_force * velocity, 0)), evaporation])
    deposit = jnp.einsum('kbp,fbp->bfk', weights, sources, precision=lax.Precision.HIGHEST) / node_weights() * parcel
    return (deposit, acceleration, -evaporation)

def region_rows(conserved):
    grid_nodes = conserved.reshape(6, N_REGION, 3, N_INNER, 3, EZ, 3)
    return grid_nodes.transpose(1, 3, 5, 0, 2, 4, 6).reshape(N_REGION * N_INNER * EZ, 162)

def grid_layout(rows_table):
    grid_nodes = rows_table.reshape(N_REGION, N_INNER, EZ, 6, 3, 3, 3).transpose(3, 0, 4, 1, 5, 2, 6)
    return grid_nodes.reshape(6, 3 * N_REGION, 3 * N_INNER, 3 * EZ)

def reference(density, momentum, energy, fuel_density, drop_pos, drop_vel, drop_mass, block_cell, block_count):
    conserved = jnp.concatenate([density[None], momentum, energy[None], fuel_density[None]], 0)
    blocks = block_cell.shape[0]
    parcel = 4.0 * EZ / (NB * PB)
    region_index = (jnp.arange(blocks) // RBLK).astype(jnp.int32)
    element_ids = region_index * (N_INNER * EZ) + block_cell
    weights = lagrange_weights(drop_pos.reshape(3, blocks, PB))
    velocity = drop_vel.reshape(3, blocks, PB)
    droplet_mass = drop_mass.reshape(blocks, PB)
    live_slots = (jnp.arange(PB)[None, :] < block_count[:, None]).astype(jnp.float32)

    def section_rates(fields_now, velocity_now, mass_now):
        rows_table = region_rows(fields_now)
        block_states = rows_table[element_ids].reshape(blocks, 6, 27)
        deposit, acceleration, mass_rate = droplet_terms(block_states, weights, velocity_now, mass_now, live_slots, parcel)
        summed = jax.ops.segment_sum(deposit.reshape(blocks, 162), element_ids, num_segments=rows_table.shape[0])
        return (fluid_tendency(fields_now) + grid_layout(summed), acceleration, mass_rate)
    rate_first, accel_first, shrink_first = section_rates(conserved, velocity, droplet_mass)
    fields_one = conserved + TIME_STEP * rate_first
    velocity_one = velocity + TIME_STEP * accel_first
    mass_one = droplet_mass + TIME_STEP * shrink_first
    rate_second, accel_second, shrink_second = section_rates(fields_one, velocity_one, mass_one)
    gas_state = 0.5 * conserved + 0.5 * (fields_one + TIME_STEP * rate_second)
    velocity_two = 0.5 * velocity + 0.5 * (velocity_one + TIME_STEP * accel_second)
    mass_two = 0.5 * droplet_mass + 0.5 * (mass_one + TIME_STEP * shrink_second)
    return (gas_state, velocity_two.reshape(3, -1), mass_two.reshape(-1))
```

```python
import functools

import jax
import jax.numpy as jnp
import numpy as np
from jax import lax
from jax.experimental import pallas as pl
from jax.experimental.pallas import tpu as pltpu
from jax.sharding import PartitionSpec as P

PB = 32
CAP = 8
GAMMA = 1.4
TIME_STEP = 0.05
EVAP_RATE = 0.5
LATENT = 0.5
LANES = 128
NODES = 32
SENT = 5 * NODES
WIDE = 256
STRIDES = (3, 1, 9)
F32, BF16 = jnp.float32, jnp.bfloat16
MESH = pl.DeviceIdType.MESH


def derivative_rows():
    line = np.array([[-1.5, 2.0, -0.5], [-0.5, 0.0, 0.5], [0.5, -2.0, 1.5]])
    table = np.zeros((NODES, 3 * NODES))
    for node in range(27):
        for d, stride in enumerate(STRIDES):
            place = node // stride % 3
            for j in range(3):
                table[node, d * NODES + node + (j - place) * stride] = -line[place, j]
    return np.concatenate([table, table], 1).astype(np.float32)


def node_scale():
    q = np.array([1.0 / 3.0, 4.0 / 3.0, 1.0 / 3.0])
    table = np.zeros((NODES, LANES), np.float32)
    for node in range(27):
        table[node] = 1.0 / (q[node // 3 % 3] * q[node % 3] * q[node // 9])
    return table


def halves(value):
    high = value.astype(BF16)
    return high, (value - high.astype(F32)).astype(BF16)


def nt_dot(left, right):
    return lax.dot_general(left, right, (((1,), (1,)), ((), ())), preferred_element_type=F32)


def field(value, f):
    return value[NODES * f : NODES * (f + 1)]


def flux_parts(value):
    inverse = 1.0 / field(value, 0)
    speeds = [field(value, 1 + c) * inverse for c in range(3)]
    kinetic = sum(field(value, 1 + c) * speeds[c] for c in range(3))
    pressure = (GAMMA - 1.0) * (field(value, 5) - 0.5 * kinetic)
    sound = jnp.sqrt(GAMMA * pressure * inverse)
    return speeds, pressure, sound


def flux_rows(value, parts, d):
    speeds, pressure, _ = parts
    speed = speeds[d]
    rows = [field(value, 1 + d)]
    for c in range(3):
        row = field(value, 1 + c) * speed
        rows.append(row + pressure if c == d else row)
    rows.append(field(value, 4) * speed)
    rows.append((field(value, 5) + pressure) * speed)
    return rows


def gas_kernel(
    elements, parcel,
    fields_ref, ids_ref, slot_ref, live_ref, pos_ref, vel_ref, mass_ref, deriv_ref, scale_ref,
    gas_out, vel_out, mass_out,
    fields_one, tend, flux_scr, weights, drop_hot, cell_hot,
    ids_in, states_out, states_in, dep_out, dep_in, low_in, high_in, dep_acc, vel_one, mass_one,
    ids_sems, state_sems, dep_sems, halo_send, halo_recv,
):
    n_inner, n_region = lax.axis_size("inner"), lax.axis_size("region")
    me, my_region = lax.axis_index("inner"), lax.axis_index("region")
    slots = n_inner * CAP
    drops = pos_ref.shape[1]
    chunk = min(512, drops)
    inner_low, inner_high = lax.rem(me + n_inner - 1, n_inner), lax.rem(me + 1, n_inner)
    region_low = lax.rem(my_region + n_region - 1, n_region)
    region_high = lax.rem(my_region + 1, n_region)

    def peer_of(j):
        return lax.rem(me + j, n_inner)

    barrier = pltpu.get_barrier_semaphore()

    @pl.loop(1, n_inner)
    def _(j):
        pl.semaphore_signal(barrier, inc=1, device_id=(my_region, peer_of(j)), device_id_type=MESH)

    region_peers = [region_high] if n_region == 2 else [region_low, region_high]
    for other in region_peers:
        pl.semaphore_signal(barrier, inc=1, device_id=(other, me), device_id_type=MESH)

    row = lax.broadcasted_iota(jnp.int32, (NODES, drops), 0)

    def basis(d, place):
        t = pos_ref[d : d + 1, :]
        first, mid, last = 0.5 * t * (t - 1.0), 1.0 - t * t, 0.5 * t * (t + 1.0)
        return jnp.where(place == 0, first, jnp.where(place == 1, mid, last))

    product = basis(0, row // 3 % 3) * basis(1, row % 3) * basis(2, row // 9)
    weights[...] = jnp.where(row < 27, product, 0.0)
    hot_row = lax.broadcasted_iota(jnp.int32, (slots, drops), 0).astype(F32)
    hot = (hot_row == slot_ref[0:1, :]).astype(F32).astype(BF16)
    drop_hot[0:slots, :] = hot
    drop_hot[slots : 2 * slots, :] = hot

    pl.semaphore_wait(barrier, n_inner - 1 + len(region_peers))

    def exchange(src, dst, sems):
        @pl.loop(1, n_inner)
        def _(j):
            peer = peer_of(j)
            pltpu.make_async_remote_copy(
                src_ref=src.at[peer], dst_ref=dst.at[me],
                send_sem=sems.at[0], recv_sem=sems.at[1],
                device_id=(my_region, peer), device_id_type=MESH,
            ).start()

    def whole(src, dst, sems):
        part = pl.ds(0, n_inner - 1)
        return pltpu.make_async_remote_copy(
            src_ref=src.at[part], dst_ref=dst.at[part],
            send_sem=sems.at[0], recv_sem=sems.at[1],
            device_id=(my_region, inner_high), device_id_type=MESH,
        )

    exchange(ids_ref, ids_in, ids_sems)
    ids_in[me] = ids_ref[me]

    lane = lax.broadcasted_iota(jnp.int32, (SENT, LANES), 1)
    node = lax.broadcasted_iota(jnp.int32, (6 * NODES, LANES), 0) % NODES

    def halo_copies(section, src):
        copies = [
            (src, high_in.at[section, 1], 0, (my_region, inner_low)),
            (src, low_in.at[section, 1], 1, (my_region, inner_high)),
            (src, high_in.at[section, 0], 2, (region_low, me)),
        ]
        if n_region != 2:
            copies.append((src, low_in.at[section, 0], 3, (region_high, me)))
        return [
            pltpu.make_async_remote_copy(
                src_ref=a, dst_ref=b, send_sem=halo_send.at[section, i],
                recv_sem=halo_recv.at[section, i], device_id=dev, device_id_type=MESH,
            )
            for a, b, i, dev in copies
        ]

    def lifts(value, parts, low, high, d):
        stride = STRIDES[d]
        place = node // stride % 3
        first, last = (place == 0) & (node < 27), (place == 2) & (node < 27)
        rows = 6 * NODES
        beyond = jnp.where(
            first, pltpu.roll(low, rows - 2 * stride, 0),
            jnp.where(last, pltpu.roll(high, 2 * stride, 0), value),
        )
        other = flux_parts(beyond)
        wave = 1.5 * jnp.maximum(
            jnp.abs(parts[0][d]) + parts[2], jnp.abs(other[0][d]) + other[2]
        )
        sign = jnp.where(first, 1.5, -1.5)[0:NODES]
        here, there = flux_rows(value, parts, d), flux_rows(beyond, other, d)
        return [
            sign * (there[f] - here[f]) + wave * (field(beyond, f) - field(value, f))
            for f in range(6)
        ]

    def section_rates(section, src, vel_src, mass_src, finish_drops):
        value = src[...]
        asked = jnp.where(lane < elements, value[0:SENT], 0.0)
        rows = nt_dot(cell_hot[...], jnp.concatenate(halves(asked), 1))
        states_out[section, :, :, 0:SENT] = rows.reshape(n_inner, CAP, SENT)
        exchange(states_out.at[section], states_in.at[section], state_sems.at[section])
        states_in[section, me] = states_out[section, me]
        halos = halo_copies(section, src)
        for copy in halos:
            copy.start()

        parts = flux_parts(value)
        for d in range(3):
            for f, part in enumerate(flux_rows(value, parts, d)):
                flux_scr[NODES * d : NODES * (d + 1), LANES * f : LANES * (f + 1)] = part
        volume = jnp.dot(
            deriv_ref[...].astype(BF16), jnp.concatenate(halves(flux_scr[...]), 0),
            preferred_element_type=F32,
        )
        along = lifts(value, parts, pltpu.roll(value, 1, 1), pltpu.roll(value, LANES - 1, 1), 2)
        for f in range(6):
            tend[NODES * f : NODES * (f + 1), :] = (
                volume[:, LANES * f : LANES * (f + 1)] + along[f]
            )

        whole(states_out.at[section], states_in.at[section], state_sems.at[section]).wait_recv()
        states = states_in[section].reshape(slots, WIDE).T[0:SENT]
        states_two = jnp.concatenate(halves(states), 1)
        dep_acc[...] = jnp.zeros_like(dep_acc)

        @pl.loop(0, drops // chunk)
        def _(i):
            at = pl.ds(pl.multiple_of(i * chunk, chunk), chunk)
            spread = jnp.dot(states_two, drop_hot[:, at], preferred_element_type=F32)
            w = weights[:, at]
            gas = [jnp.sum(field(spread, f) * w, 0, keepdims=True) for f in range(5)]
            inverse = 1.0 / gas[0]
            vel = [vel_src[c : c + 1, at] for c in range(3)]
            mass, live = mass_src[0:1, at], live_ref[0:1, at]
            rel = [gas[1 + c] * inverse - vel[c] for c in range(3)]
            cube_root = jnp.exp(jnp.log(mass) * (1.0 / 3.0))
            drag = live / (cube_root * cube_root)
            accel = [drag * rel[c] for c in range(3)]
            evap = (
                live * EVAP_RATE * cube_root
                * jnp.sqrt(1.0 + (rel[0] * rel[0] + rel[1] * rel[1] + rel[2] * rel[2]))
                * (1.0 - gas[4] * inverse)
            )
            force = [mass * accel[c] for c in range(3)]
            work = sum(force[c] * vel[c] for c in range(3))
            square = sum(vel[c] * vel[c] for c in range(3))
            sources = [evap] + [evap * vel[c] - force[c] for c in range(3)]
            sources.append(evap * (LATENT + 0.5 * square) - work)
            placed = jnp.concatenate([w * s for s in sources], 0)
            dep_acc[...] += nt_dot(jnp.concatenate(halves(placed), 0), drop_hot[0:slots, at])
            finish_drops(at, vel, mass, accel, evap)

        summed = dep_acc[0:SENT, :] + dep_acc[SENT : 2 * SENT, :]
        dep_out[section, :, :, 0:SENT] = summed.T.reshape(n_inner, CAP, SENT)
        exchange(dep_out.at[section], dep_in.at[section], dep_sems.at[section])
        dep_in[section, me] = dep_out[section, me]

        for copy in halos:
            copy.wait_recv()
        low_x = high_in[section, 0] if n_region == 2 else low_in[section, 0]
        along_x = lifts(value, parts, low_x, high_in[section, 0], 0)
        along_y = lifts(value, parts, low_in[section, 1], high_in[section, 1], 1)
        for f in range(6):
            tend[NODES * f : NODES * (f + 1), :] += along_x[f] + along_y[f]

        whole(dep_out.at[section], dep_in.at[section], dep_sems.at[section]).wait_recv()
        deposits = dep_in[section].reshape(slots, WIDE).T[0:SENT]
        arrived = jnp.dot(
            jnp.concatenate(halves(deposits), 0), cell_hot[:, 0:LANES], preferred_element_type=F32
        )
        arrived = arrived[0:SENT] + arrived[SENT : 2 * SENT]
        scale = scale_ref[...] * parcel
        rates = []
        for f, source in enumerate((0, 1, 2, 3, 0, 4)):
            rates.append(
                tend[NODES * f : NODES * (f + 1), :] + scale * field(arrived, source)
            )
        return value, rates, halos

    def drops_first(at, vel, mass, accel, evap):
        for c in range(3):
            vel_one[c : c + 1, at] = vel[c] + TIME_STEP * accel[c]
        mass_one[0:1, at] = mass - TIME_STEP * evap

    def drops_second(at, vel, mass, accel, evap):
        for c in range(3):
            vel_out[c : c + 1, at] = 0.5 * vel_ref[c : c + 1, at] + 0.5 * (
                vel[c] + TIME_STEP * accel[c]
            )
        mass_out[0:1, at] = 0.5 * mass_ref[0:1, at] + 0.5 * (mass - TIME_STEP * evap)

    whole(ids_ref, ids_in, ids_sems).wait_recv()
    lane_id = lax.broadcasted_iota(jnp.int32, (slots, LANES), 1).astype(F32)
    own = (ids_in[...].reshape(slots, LANES) == element_of(lane_id, elements)).astype(F32).astype(BF16)
    cell_hot[:, 0:LANES] = own
    cell_hot[:, LANES : 2 * LANES] = own

    value, rates, halos_one = section_rates(0, fields_ref, vel_ref, mass_ref, drops_first)
    for f in range(6):
        fields_one[NODES * f : NODES * (f + 1), :] = field(value, f) + TIME_STEP * rates[f]
    value, rates, halos_two = section_rates(1, fields_one, vel_one, mass_one, drops_second)
    for f in range(6):
        gas_out[NODES * f : NODES * (f + 1), :] = 0.5 * fields_ref[
            NODES * f : NODES * (f + 1), :
        ] + 0.5 * (field(value, f) + TIME_STEP * rates[f])

    whole(ids_ref, ids_in, ids_sems).wait_send()
    for section in range(2):
        whole(states_out.at[section], states_in.at[section], state_sems.at[section]).wait_send()
        whole(dep_out.at[section], dep_in.at[section], dep_sems.at[section]).wait_send()
    for copy in halos_one + halos_two:
        copy.wait_send()


def lane_split(elements):
    assert elements <= LANES <= 3 * elements
    return (LANES - elements) // 2


def element_of(lane_id, elements):
    extra = lane_split(elements)
    return jnp.where(
        lane_id < elements, lane_id,
        jnp.where(lane_id < elements + extra, lane_id - elements, lane_id - (LANES - elements)),
    )


def on_device(
    density, momentum, energy, fuel_density, drop_pos, drop_vel, drop_mass, block_cell, block_count
):
    n_inner = lax.axis_size("inner")
    fields = jnp.concatenate([density[None], momentum, fuel_density[None], energy[None]], 0)
    elements = fields.shape[3] // 3
    blocks = block_cell.shape[0]
    drops = blocks * PB
    slots = n_inner * CAP
    parcel = 4.0 * elements / drops
    extra = lane_split(elements)

    table = fields.reshape(6, 3, 3, elements, 3).transpose(0, 4, 1, 2, 3).reshape(6, 27, elements)
    table = jnp.concatenate([table, table[:, : NODES - 27]], 1)
    table = jnp.concatenate(
        [table, table[:, :, :extra], table[:, :, 2 * elements + extra - LANES :]], 2
    ).reshape(6 * NODES, LANES)

    owner = block_cell // elements
    earlier = jnp.sum((owner[None, :] < owner[:, None]).astype(jnp.int32), 1)
    slot = owner * CAP + jnp.arange(blocks, dtype=jnp.int32) - earlier
    local = block_cell - owner * elements
    taken = slot[None, :] == jnp.arange(slots, dtype=jnp.int32)[:, None]
    ids = (jnp.sum(jnp.where(taken, local[None, :] + 1, 0), 1) - 1).astype(F32)
    ids = jnp.broadcast_to(ids.reshape(n_inner, CAP, 1), (n_inner, CAP, LANES))
    live = (jnp.arange(PB)[None, :] < block_count[:, None]).astype(F32).reshape(1, drops)
    drop_slot = jnp.repeat(slot.astype(F32), PB).reshape(1, drops)

    vmem = pl.BlockSpec(memory_space=pltpu.VMEM)
    gas, vel, mass = pl.pallas_call(
        functools.partial(gas_kernel, elements, parcel),
        out_shape=(
            jax.ShapeDtypeStruct((6 * NODES, LANES), F32),
            jax.ShapeDtypeStruct((3, drops), F32),
            jax.ShapeDtypeStruct((1, drops), F32),
        ),
        in_specs=[vmem] * 9,
        out_specs=(vmem, vmem, vmem),
        scratch_shapes=[
            pltpu.VMEM((6 * NODES, LANES), F32),
            pltpu.VMEM((6 * NODES, LANES), F32),
            pltpu.VMEM((3 * NODES, 6 * LANES), F32),
            pltpu.VMEM((NODES, drops), F32),
            pltpu.VMEM((2 * slots, drops), BF16),
            pltpu.VMEM((slots, 2 * LANES), BF16),
            pltpu.VMEM((n_inner, CAP, LANES), F32),
            pltpu.VMEM((2, n_inner, CAP, WIDE), F32),
            pltpu.VMEM((2, n_inner, CAP, WIDE), F32),
            pltpu.VMEM((2, n_inner, CAP, WIDE), F32),
            pltpu.VMEM((2, n_inner, CAP, WIDE), F32),
            pltpu.VMEM((2, 2, 6 * NODES, LANES), F32),
            pltpu.VMEM((2, 2, 6 * NODES, LANES), F32),
            pltpu.VMEM((2 * SENT, slots), F32),
            pltpu.VMEM((3, drops), F32),
            pltpu.VMEM((1, drops), F32),
            pltpu.SemaphoreType.DMA((2,)),
            pltpu.SemaphoreType.DMA((2, 2)),
            pltpu.SemaphoreType.DMA((2, 2)),
            pltpu.SemaphoreType.DMA((2, 4)),
            pltpu.SemaphoreType.DMA((2, 4)),
        ],
        compiler_params=pltpu.CompilerParams(
            collective_id=0, has_side_effects=True, vmem_limit_bytes=48 * 1024 * 1024
        ),
    )(
        table, ids, drop_slot, live, drop_pos, drop_vel, drop_mass.reshape(1, drops),
        jnp.asarray(derivative_rows()), jnp.asarray(node_scale()),
    )
    gas = gas.reshape(6, NODES, LANES)[:, :27, :elements].reshape(6, 3, 3, 3, elements)
    gas = gas.transpose(0, 2, 3, 4, 1).reshape(6, 3, 3, 3 * elements)
    gas = jnp.concatenate([gas[:4], gas[5:6], gas[4:5]], 0)
    return gas, vel, mass.reshape(drops)


def solution(mesh):
    placed = (
        P("region", "inner", None),
        P(None, "region", "inner", None),
        P("region", "inner", None),
        P("region", "inner", None),
        P(None, ("region", "inner")),
        P(None, ("region", "inner")),
        P(("region", "inner")),
        P(("region", "inner")),
        P(("region", "inner")),
    )
    return jax.shard_map(
        on_device,
        mesh=mesh,
        in_specs=placed,
        out_specs=(
            P(None, "region", "inner", None),
            P(None, ("region", "inner")),
            P(("region", "inner")),
        ),
        check_vma=False,
    )
```

```python
import functools

import jax
import jax.numpy as jnp
import numpy as np
from jax import lax
from jax.experimental import pallas as pl
from jax.experimental.pallas import tpu as pltpu
from jax.sharding import PartitionSpec as P

PB = 32
CAP = 8
GAMMA = 1.4
TIME_STEP = 0.05
EVAP_RATE = 0.5
LATENT = 0.5
LANES = 128
NODES = 32
SENT = 5 * NODES
WIDE = 256
STRIDES = (3, 1, 9)
F32, BF16 = jnp.float32, jnp.bfloat16
MESH = pl.DeviceIdType.MESH


def derivative_rows():
    line = np.array([[-1.5, 2.0, -0.5], [-0.5, 0.0, 0.5], [0.5, -2.0, 1.5]])
    table = np.zeros((NODES, 3 * NODES))
    for node in range(27):
        for d, stride in enumerate(STRIDES):
            place = node // stride % 3
            for j in range(3):
                table[node, d * NODES + node + (j - place) * stride] = -line[place, j]
    return np.concatenate([table, table], 1).astype(np.float32)


def node_scale():
    q = np.array([1.0 / 3.0, 4.0 / 3.0, 1.0 / 3.0])
    table = np.zeros((NODES, LANES), np.float32)
    for node in range(27):
        table[node] = 1.0 / (q[node // 3 % 3] * q[node % 3] * q[node // 9])
    return table


def halves(value):
    high = value.astype(BF16)
    return high, (value - high.astype(F32)).astype(BF16)


def thirds(value):
    high = value.astype(BF16)
    rest = value - high.astype(F32)
    return (high,) + halves(rest)


def nt_dot(left, right):
    return lax.dot_general(left, right, (((1,), (1,)), ((), ())), preferred_element_type=F32)


def field(value, f):
    return value[NODES * f : NODES * (f + 1)]


def flux_parts(value):
    inverse = 1.0 / field(value, 0)
    speeds = [field(value, 1 + c) * inverse for c in range(3)]
    kinetic = sum(field(value, 1 + c) * speeds[c] for c in range(3))
    pressure = (GAMMA - 1.0) * (field(value, 5) - 0.5 * kinetic)
    sound = jnp.sqrt(GAMMA * pressure * inverse)
    return speeds, pressure, sound


def flux_rows(value, parts, d):
    speeds, pressure, _ = parts
    speed = speeds[d]
    rows = [field(value, 1 + d)]
    for c in range(3):
        row = field(value, 1 + c) * speed
        rows.append(row + pressure if c == d else row)
    rows.append(field(value, 4) * speed)
    rows.append((field(value, 5) + pressure) * speed)
    return rows


def gas_kernel(
    elements, parcel,
    density_ref, momentum_ref, energy_ref, fuel_ref, pos_ref, vel_ref, mass_ref, cell_ref,
    count_ref, deriv_ref, scale_ref,
    gas_out, vel_out, mass_out,
    natural, fields_ref, ids_ref, live_ref, pick, fields_one, tend, flux_scr, weights, drop_hot, cell_hot,
    ids_in, states_out, states_in, dep_out, dep_in, low_in, high_in, dep_acc, vel_one, mass_one, by_lane,
    ids_sems, state_sems, dep_sems, halo_send, halo_recv,
):
    n_inner, n_region = lax.axis_size("inner"), lax.axis_size("region")
    me, my_region = lax.axis_index("inner"), lax.axis_index("region")
    slots = n_inner * CAP
    drops = pos_ref.shape[1]
    chunk = min(512, drops)
    inner_low, inner_high = lax.rem(me + n_inner - 1, n_inner), lax.rem(me + 1, n_inner)
    region_low = lax.rem(my_region + n_region - 1, n_region)
    region_high = lax.rem(my_region + 1, n_region)

    def peer_of(j):
        return lax.rem(me + j, n_inner)

    barrier = pltpu.get_barrier_semaphore()

    @pl.loop(1, n_inner)
    def _(j):
        pl.semaphore_signal(barrier, inc=1, device_id=(my_region, peer_of(j)), device_id_type=MESH)

    region_peers = [region_high] if n_region == 2 else [region_low, region_high]
    for other in region_peers:
        pl.semaphore_signal(barrier, inc=1, device_id=(other, me), device_id_type=MESH)

    blocks = cell_ref.shape[1]
    cell = cell_ref[...].astype(F32)
    owner = jnp.floor((cell + 0.5) * (1.0 / elements))
    local = cell - owner * elements
    square = (blocks, blocks)
    across = jnp.broadcast_to(owner, square)
    diagonal = lax.broadcasted_iota(jnp.int32, square, 0) == lax.broadcasted_iota(
        jnp.int32, square, 1
    )
    down = jnp.sum(jnp.where(diagonal, across, 0.0), 1, keepdims=True)
    earlier = jnp.sum(jnp.where(down < across, 1.0, 0.0), 0, keepdims=True)
    rank = lax.broadcasted_iota(jnp.int32, (1, blocks), 1).astype(F32) - earlier
    slot_of = lax.broadcasted_iota(jnp.int32, (slots, blocks), 0).astype(F32)
    taken = slot_of == owner * CAP + rank
    ids = jnp.sum(jnp.where(taken, local + 1.0, 0.0), 1, keepdims=True) - 1.0
    ids_ref[...] = jnp.broadcast_to(ids, (slots, LANES)).reshape(n_inner, CAP, LANES)

    pl.semaphore_wait(barrier, n_inner - 1 + len(region_peers))

    def exchange(src, dst, sems):
        @pl.loop(1, n_inner)
        def _(j):
            peer = peer_of(j)
            pltpu.make_async_remote_copy(
                src_ref=src.at[peer], dst_ref=dst.at[me],
                send_sem=sems.at[0], recv_sem=sems.at[1],
                device_id=(my_region, peer), device_id_type=MESH,
            ).start()

    def whole(src, dst, sems):
        part = pl.ds(0, n_inner - 1)
        return pltpu.make_async_remote_copy(
            src_ref=src.at[part], dst_ref=dst.at[part],
            send_sem=sems.at[0], recv_sem=sems.at[1],
            device_id=(my_region, inner_high), device_id_type=MESH,
        )

    exchange(ids_ref, ids_in, ids_sems)
    ids_in[me] = ids_ref[me]

    for x in range(3):
        for f in range(6):
            part = (density_ref, momentum_ref, momentum_ref, momentum_ref, fuel_ref, energy_ref)[f]
            natural[9 * f + 3 * x : 9 * f + 3 * x + 3, :] = (
                part[f - 1, x] if 1 <= f <= 3 else part[x]
            )
    length = 3 * elements
    node_z = lax.broadcasted_iota(jnp.int32, (length, LANES), 0)
    pick_lane = lax.broadcasted_iota(jnp.int32, (length, LANES), 1)
    first_node = 3 * element_of(pick_lane, elements)
    for c in range(3):
        chosen = (node_z == first_node + c).astype(F32)
        pick[:, LANES * c : LANES * (c + 1)] = chosen.astype(BF16)
    for_lanes = sum(
        jnp.dot(part, pick[...], preferred_element_type=F32) for part in thirds(natural[...])
    )
    for c in range(3):
        for f in range(6):
            rows = for_lanes[9 * f : 9 * f + 9, LANES * c : LANES * (c + 1)]
            fields_ref[NODES * f + 9 * c : NODES * f + 9 * c + 9, :] = rows
            if c == 0:
                fields_ref[NODES * f + 27 : NODES * (f + 1), :] = rows[0 : NODES - 27]

    row = lax.broadcasted_iota(jnp.int32, (NODES, drops), 0)

    def basis(d, place):
        t = pos_ref[d : d + 1, :]
        first, mid, last = 0.5 * t * (t - 1.0), 1.0 - t * t, 0.5 * t * (t + 1.0)
        return jnp.where(place == 0, first, jnp.where(place == 1, mid, last))

    product = basis(0, row // 3 % 3) * basis(1, row % 3) * basis(2, row // 9)
    weights[...] = jnp.where(row < 27, product, 0.0)
    in_block = lax.broadcasted_iota(jnp.int32, (blocks, drops), 1) // PB
    block_row = lax.broadcasted_iota(jnp.int32, (blocks, drops), 0)
    which = lax.broadcasted_iota(jnp.int32, (16, blocks), 0)
    wanted = jnp.where(
        which == 0, owner, jnp.where(which == 1, rank, count_ref[...].astype(F32))
    ).astype(BF16)
    spread = jnp.dot(
        wanted, (in_block == block_row).astype(F32).astype(BF16), preferred_element_type=F32
    )
    turn = (lax.broadcasted_iota(jnp.int32, (1, drops), 1) % PB).astype(F32)
    live_ref[...] = jnp.where(turn < spread[2:3], 1.0, 0.0)
    hot_row = lax.broadcasted_iota(jnp.int32, (slots, drops), 0).astype(F32)
    hot = (hot_row == spread[0:1] * CAP + spread[1:2]).astype(F32).astype(BF16)
    drop_hot[0:slots, :] = hot
    drop_hot[slots : 2 * slots, :] = hot

    lane = lax.broadcasted_iota(jnp.int32, (SENT, LANES), 1)
    node = lax.broadcasted_iota(jnp.int32, (6 * NODES, LANES), 0) % NODES

    def halo_copies(section, src):
        copies = [
            (src, high_in.at[section, 1], 0, (my_region, inner_low)),
            (src, low_in.at[section, 1], 1, (my_region, inner_high)),
            (src, high_in.at[section, 0], 2, (region_low, me)),
        ]
        if n_region != 2:
            copies.append((src, low_in.at[section, 0], 3, (region_high, me)))
        return [
            pltpu.make_async_remote_copy(
                src_ref=a, dst_ref=b, send_sem=halo_send.at[section, i],
                recv_sem=halo_recv.at[section, i], device_id=dev, device_id_type=MESH,
            )
            for a, b, i, dev in copies
        ]

    def lifts(value, parts, low, high, d):
        stride = STRIDES[d]
        place = node // stride % 3
        first, last = (place == 0) & (node < 27), (place == 2) & (node < 27)
        rows = 6 * NODES
        beyond = jnp.where(
            first, pltpu.roll(low, rows - 2 * stride, 0),
            jnp.where(last, pltpu.roll(high, 2 * stride, 0), value),
        )
        other = flux_parts(beyond)
        wave = 1.5 * jnp.maximum(
            jnp.abs(parts[0][d]) + parts[2], jnp.abs(other[0][d]) + other[2]
        )
        sign = jnp.where(first, 1.5, -1.5)[0:NODES]
        here, there = flux_rows(value, parts, d), flux_rows(beyond, other, d)
        return [
            sign * (there[f] - here[f]) + wave * (field(beyond, f) - field(value, f))
            for f in range(6)
        ]

    def section_rates(section, src, vel_src, mass_src, finish_drops):
        value = src[...]
        asked = jnp.where(lane < elements, value[0:SENT], 0.0)
        rows = nt_dot(cell_hot[...], jnp.concatenate(halves(asked), 1))
        states_out[section, :, :, 0:SENT] = rows.reshape(n_inner, CAP, SENT)
        exchange(states_out.at[section], states_in.at[section], state_sems.at[section])
        states_in[section, me] = states_out[section, me]
        halos = halo_copies(section, src)
        for copy in halos:
            copy.start()

        parts = flux_parts(value)
        for d in range(3):
            for f, part in enumerate(flux_rows(value, parts, d)):
                flux_scr[NODES * d : NODES * (d + 1), LANES * f : LANES * (f + 1)] = part
        volume = jnp.dot(
            deriv_ref[...].astype(BF16), jnp.concatenate(halves(flux_scr[...]), 0),
            preferred_element_type=F32,
        )
        along = lifts(value, parts, pltpu.roll(value, 1, 1), pltpu.roll(value, LANES - 1, 1), 2)
        for f in range(6):
            tend[NODES * f : NODES * (f + 1), :] = (
                volume[:, LANES * f : LANES * (f + 1)] + along[f]
            )

        whole(states_out.at[section], states_in.at[section], state_sems.at[section]).wait_recv()
        states = states_in[section].reshape(slots, WIDE).T[0:SENT]
        states_two = jnp.concatenate(halves(states), 1)
        dep_acc[...] = jnp.zeros_like(dep_acc)

        @pl.loop(0, drops // chunk)
        def _(i):
            at = pl.ds(pl.multiple_of(i * chunk, chunk), chunk)
            spread = jnp.dot(states_two, drop_hot[:, at], preferred_element_type=F32)
            w = weights[:, at]
            gas = [jnp.sum(field(spread, f) * w, 0, keepdims=True) for f in range(5)]
            inverse = 1.0 / gas[0]
            vel = [vel_src[c : c + 1, at] for c in range(3)]
            mass, live = mass_src[0:1, at], live_ref[0:1, at]
            rel = [gas[1 + c] * inverse - vel[c] for c in range(3)]
            cube_root = jnp.exp(jnp.log(mass) * (1.0 / 3.0))
            drag = live / (cube_root * cube_root)
            accel = [drag * rel[c] for c in range(3)]
            evap = (
                live * EVAP_RATE * cube_root
                * jnp.sqrt(1.0 + (rel[0] * rel[0] + rel[1] * rel[1] + rel[2] * rel[2]))
                * (1.0 - gas[4] * inverse)
            )
            force = [mass * accel[c] for c in range(3)]
            work = sum(force[c] * vel[c] for c in range(3))
            square = sum(vel[c] * vel[c] for c in range(3))
            sources = [evap] + [evap * vel[c] - force[c] for c in range(3)]
            sources.append(evap * (LATENT + 0.5 * square) - work)
            placed = jnp.concatenate([w * s for s in sources], 0)
            dep_acc[...] += nt_dot(jnp.concatenate(halves(placed), 0), drop_hot[0:slots, at])
            finish_drops(at, vel, mass, accel, evap)

        summed = dep_acc[0:SENT, :] + dep_acc[SENT : 2 * SENT, :]
        dep_out[section, :, :, 0:SENT] = summed.T.reshape(n_inner, CAP, SENT)
        exchange(dep_out.at[section], dep_in.at[section], dep_sems.at[section])
        dep_in[section, me] = dep_out[section, me]

        for copy in halos:
            copy.wait_recv()
        low_x = high_in[section, 0] if n_region == 2 else low_in[section, 0]
        along_x = lifts(value, parts, low_x, high_in[section, 0], 0)
        along_y = lifts(value, parts, low_in[section, 1], high_in[section, 1], 1)
        for f in range(6):
            tend[NODES * f : NODES * (f + 1), :] += along_x[f] + along_y[f]

        whole(dep_out.at[section], dep_in.at[section], dep_sems.at[section]).wait_recv()
        deposits = dep_in[section].reshape(slots, WIDE).T[0:SENT]
        arrived = jnp.dot(
            jnp.concatenate(halves(deposits), 0), cell_hot[:, 0:LANES], preferred_element_type=F32
        )
        arrived = arrived[0:SENT] + arrived[SENT : 2 * SENT]
        scale = scale_ref[...] * parcel
        rates = []
        for f, source in enumerate((0, 1, 2, 3, 0, 4)):
            rates.append(
                tend[NODES * f : NODES * (f + 1), :] + scale * field(arrived, source)
            )
        return value, rates, halos

    def drops_first(at, vel, mass, accel, evap):
        for c in range(3):
            vel_one[c : c + 1, at] = vel[c] + TIME_STEP * accel[c]
        mass_one[0:1, at] = mass - TIME_STEP * evap

    def drops_second(at, vel, mass, accel, evap):
        for c in range(3):
            vel_out[c : c + 1, at] = 0.5 * vel_ref[c : c + 1, at] + 0.5 * (
                vel[c] + TIME_STEP * accel[c]
            )
        mass_out[0:1, at] = 0.5 * mass_ref[0:1, at] + 0.5 * (mass - TIME_STEP * evap)

    whole(ids_ref, ids_in, ids_sems).wait_recv()
    lane_id = lax.broadcasted_iota(jnp.int32, (slots, LANES), 1).astype(F32)
    own = (ids_in[...].reshape(slots, LANES) == element_of(lane_id, elements)).astype(F32).astype(BF16)
    cell_hot[:, 0:LANES] = own
    cell_hot[:, LANES : 2 * LANES] = own

    value, rates, halos_one = section_rates(0, fields_ref, vel_ref, mass_ref, drops_first)
    for f in range(6):
        fields_one[NODES * f : NODES * (f + 1), :] = field(value, f) + TIME_STEP * rates[f]
    value, rates, halos_two = section_rates(1, fields_one, vel_one, mass_one, drops_second)
    own_lane = lax.broadcasted_iota(jnp.int32, (NODES, LANES), 1) < elements
    for f in range(6):
        whole_rows = slice(NODES * f, NODES * (f + 1))
        final = 0.5 * fields_ref[whole_rows, :] + 0.5 * (field(value, f) + TIME_STEP * rates[f])
        final = jnp.where(own_lane, final, 0.0)
        for c in range(3):
            by_lane[9 * f : 9 * f + 9, LANES * c : LANES * (c + 1)] = final[9 * c : 9 * c + 9]
    grid = sum(nt_dot(part, pick[...]) for part in thirds(by_lane[...]))
    for f, target in enumerate((0, 1, 2, 3, 5, 4)):
        for x in range(3):
            gas_out[target, x] = grid[9 * f + 3 * x : 9 * f + 3 * x + 3]

    whole(ids_ref, ids_in, ids_sems).wait_send()
    for section in range(2):
        whole(states_out.at[section], states_in.at[section], state_sems.at[section]).wait_send()
        whole(dep_out.at[section], dep_in.at[section], dep_sems.at[section]).wait_send()
    for copy in halos_one + halos_two:
        copy.wait_send()


def lane_split(elements):
    assert elements <= LANES <= 3 * elements
    return (LANES - elements) // 2


def element_of(lane_id, elements):
    extra = lane_split(elements)
    return jnp.where(
        lane_id < elements, lane_id,
        jnp.where(lane_id < elements + extra, lane_id - elements, lane_id - (LANES - elements)),
    )


def on_device(
    density, momentum, energy, fuel_density, drop_pos, drop_vel, drop_mass, block_cell, block_count
):
    n_inner = lax.axis_size("inner")
    elements = density.shape[2] // 3
    blocks = block_cell.shape[0]
    drops = blocks * PB
    slots = n_inner * CAP
    parcel = 4.0 * elements / drops

    vmem = pl.BlockSpec(memory_space=pltpu.VMEM)
    gas, vel, mass = pl.pallas_call(
        functools.partial(gas_kernel, elements, parcel),
        out_shape=(
            jax.ShapeDtypeStruct((6, 3, 3, 3 * elements), F32),
            jax.ShapeDtypeStruct((3, drops), F32),
            jax.ShapeDtypeStruct((1, drops), F32),
        ),
        in_specs=[vmem] * 11,
        out_specs=(vmem, vmem, vmem),
        scratch_shapes=[
            pltpu.VMEM((54, 3 * elements), F32),
            pltpu.VMEM((6 * NODES, LANES), F32),
            pltpu.VMEM((n_inner, CAP, LANES), F32),
            pltpu.VMEM((1, drops), F32),
            pltpu.VMEM((3 * elements, 3 * LANES), BF16),
            pltpu.VMEM((6 * NODES, LANES), F32),
            pltpu.VMEM((6 * NODES, LANES), F32),
            pltpu.VMEM((3 * NODES, 6 * LANES), F32),
            pltpu.VMEM((NODES, drops), F32),
            pltpu.VMEM((2 * slots, drops), BF16),
            pltpu.VMEM((slots, 2 * LANES), BF16),
            pltpu.VMEM((n_inner, CAP, LANES), F32),
            pltpu.VMEM((2, n_inner, CAP, WIDE), F32),
            pltpu.VMEM((2, n_inner, CAP, WIDE), F32),
            pltpu.VMEM((2, n_inner, CAP, WIDE), F32),
            pltpu.VMEM((2, n_inner, CAP, WIDE), F32),
            pltpu.VMEM((2, 2, 6 * NODES, LANES), F32),
            pltpu.VMEM((2, 2, 6 * NODES, LANES), F32),
            pltpu.VMEM((2 * SENT, slots), F32),
            pltpu.VMEM((3, drops), F32),
            pltpu.VMEM((1, drops), F32),
            pltpu.VMEM((54, 3 * LANES), F32),
            pltpu.SemaphoreType.DMA((2,)),
            pltpu.SemaphoreType.DMA((2, 2)),
            pltpu.SemaphoreType.DMA((2, 2)),
            pltpu.SemaphoreType.DMA((2, 4)),
            pltpu.SemaphoreType.DMA((2, 4)),
        ],
        compiler_params=pltpu.CompilerParams(
            collective_id=0, has_side_effects=True, vmem_limit_bytes=48 * 1024 * 1024
        ),
    )(
        density, momentum, energy, fuel_density, drop_pos, drop_vel, drop_mass.reshape(1, drops),
        block_cell.reshape(1, blocks), block_count.reshape(1, blocks),
        jnp.asarray(derivative_rows()), jnp.asarray(node_scale()),
    )
    return gas, vel, mass.reshape(drops)


def solution(mesh):
    placed = (
        P("region", "inner", None),
        P(None, "region", "inner", None),
        P("region", "inner", None),
        P("region", "inner", None),
        P(None, ("region", "inner")),
        P(None, ("region", "inner")),
        P(("region", "inner")),
        P(("region", "inner")),
        P(("region", "inner")),
    )
    return jax.shard_map(
        on_device,
        mesh=mesh,
        in_specs=placed,
        out_specs=(
            P(None, "region", "inner", None),
            P(None, ("region", "inner")),
            P(("region", "inner")),
        ),
        check_vma=False,
    )
```

```python
import functools

import jax
import jax.numpy as jnp
import numpy as np
from jax import lax
from jax.experimental import pallas as pl
from jax.experimental.pallas import tpu as pltpu
from jax.sharding import PartitionSpec as P

PB = 32
CAP = 8
GAMMA = 1.4
TIME_STEP = 0.05
EVAP_RATE = 0.5
LATENT = 0.5
LANES = 128
PER_LINE = LANES // PB
NODES = 32
SENT = 5 * NODES
WIDE = 256
STRIDES = (3, 1, 9)
F32, BF16 = jnp.float32, jnp.bfloat16
MESH = pl.DeviceIdType.MESH


def derivative_rows():
    line = np.array([[-1.5, 2.0, -0.5], [-0.5, 0.0, 0.5], [0.5, -2.0, 1.5]])
    table = np.zeros((NODES, 3 * NODES))
    for node in range(27):
        for d, stride in enumerate(STRIDES):
            place = node // stride % 3
            for j in range(3):
                table[node, d * NODES + node + (j - place) * stride] = -line[place, j]
    return np.concatenate([table, table], 1).astype(np.float32)


def node_scale():
    q = np.array([1.0 / 3.0, 4.0 / 3.0, 1.0 / 3.0])
    table = np.zeros((NODES, LANES), np.float32)
    for node in range(27):
        table[node] = 1.0 / (q[node // 3 % 3] * q[node % 3] * q[node // 9])
    return table


def halves(value):
    high = value.astype(BF16)
    return high, (value - high.astype(F32)).astype(BF16)


def thirds(value):
    high = value.astype(BF16)
    rest = value - high.astype(F32)
    return (high,) + halves(rest)


def nt_dot(left, right):
    return lax.dot_general(left, right, (((1,), (1,)), ((), ())), preferred_element_type=F32)


def field(value, f):
    return value[NODES * f : NODES * (f + 1)]


def flux_parts(value):
    inverse = 1.0 / field(value, 0)
    speeds = [field(value, 1 + c) * inverse for c in range(3)]
    kinetic = sum(field(value, 1 + c) * speeds[c] for c in range(3))
    pressure = (GAMMA - 1.0) * (field(value, 5) - 0.5 * kinetic)
    sound = jnp.sqrt(GAMMA * pressure * inverse)
    return speeds, pressure, sound


def flux_rows(value, parts, d):
    speeds, pressure, _ = parts
    speed = speeds[d]
    rows = [field(value, 1 + d)]
    for c in range(3):
        row = field(value, 1 + c) * speed
        rows.append(row + pressure if c == d else row)
    rows.append(field(value, 4) * speed)
    rows.append((field(value, 5) + pressure) * speed)
    return rows


def gas_kernel(
    elements, parcel,
    density_hbm, momentum_hbm, energy_hbm, fuel_hbm, pos_hbm, vel_hbm, mass_hbm, deriv_hbm,
    scale_hbm, cell_ref,
    gas_out, vel_out, mass_out,
    density_ref, momentum_ref, energy_ref, fuel_ref, pos_ref, vel_ref, mass_ref, deriv_ref,
    scale_ref,
    natural, fields_ref, pick, fields_one, tend, flux_scr, lines, packed, weights, gathered,
    deposits, drops_out, drops_in, back_out, back_in, low_in, high_in, by_lane, placed_out,
    in_sems, out_sems, back_sems, halo_send, halo_recv,
):
    n_inner, n_region = lax.axis_size("inner"), lax.axis_size("region")
    me, my_region = lax.axis_index("inner"), lax.axis_index("region")
    slots = n_inner * CAP
    blocks = cell_ref.shape[1]
    lines_n = blocks // PER_LINE
    inner_low, inner_high = lax.rem(me + n_inner - 1, n_inner), lax.rem(me + 1, n_inner)
    region_low = lax.rem(my_region + n_region - 1, n_region)
    region_high = lax.rem(my_region + 1, n_region)

    loads = [
        pltpu.make_async_copy(src, dst, in_sems.at[n])
        for n, (src, dst) in enumerate((
            (pos_hbm, pos_ref), (vel_hbm, vel_ref), (mass_hbm, mass_ref),
            (density_hbm, density_ref), (momentum_hbm, momentum_ref), (energy_hbm, energy_ref),
            (fuel_hbm, fuel_ref), (deriv_hbm, deriv_ref), (scale_hbm, scale_ref),
        ))
    ]
    for load in loads:
        load.start()

    bits = [1 << n for n in range((n_inner - 1).bit_length())]
    paired = n_inner == 1 << len(bits)

    def peer_of(j):
        if not paired:
            return lax.rem(me + j, n_inner)
        return sum((me // b % 2 + j // b % 2) % 2 * b for b in bits)

    def each_peer(body):
        if n_inner <= 16:
            for j in range(n_inner - 1, 0, -1):
                body(peer_of(j))
        else:
            @pl.loop(1, n_inner)
            def _(j):
                body(peer_of(n_inner - j))

    barrier = pltpu.get_barrier_semaphore()

    def greet(peer):
        pl.semaphore_signal(barrier, inc=1, device_id=(my_region, peer), device_id_type=MESH)

    each_peer(greet)
    region_peers = [region_high] if n_region == 2 else [region_low, region_high]
    for other in region_peers:
        pl.semaphore_signal(barrier, inc=1, device_id=(other, me), device_id_type=MESH)

    cell = cell_ref[0:1, :].astype(F32)
    owner = jnp.floor((cell + 0.5) * (1.0 / elements))
    local = cell - owner * elements
    square = (blocks, blocks)
    diagonal = lax.broadcasted_iota(jnp.int32, square, 0) == lax.broadcasted_iota(
        jnp.int32, square, 1
    )

    def upright(row):
        return jnp.sum(
            jnp.where(diagonal, jnp.broadcast_to(row, square), 0.0), 1, keepdims=True
        )

    down = upright(owner)
    earlier = jnp.sum(jnp.where(down < jnp.broadcast_to(owner, square), 1.0, 0.0), 0, keepdims=True)
    lane_b = lax.broadcasted_iota(jnp.int32, (1, blocks), 1)
    number = (lane_b % lines_n * PER_LINE + lane_b // lines_n).astype(F32)
    slot = owner * CAP + number - earlier
    taken = lax.broadcasted_iota(jnp.int32, (slots, blocks), 0).astype(F32) == slot
    taken = taken.astype(F32).astype(BF16)
    taken_up = lax.broadcasted_iota(jnp.int32, (blocks, slots), 1).astype(F32) == upright(slot)
    taken_up = taken_up.astype(F32).astype(BF16)

    for load in loads[:3]:
        load.wait()
    for q in range(7):
        src = (pos_ref, vel_ref, mass_ref)[q // 3]
        for r in range(lines_n):
            lines[q, r : r + 1, :] = src[q % 3 : q % 3 + 1, LANES * r : LANES * (r + 1)]
    for q in range(7):
        for j in range(PER_LINE):
            packed[lines_n * j : lines_n * (j + 1), PB * q : PB * (q + 1)] = lines[
                q, :, PB * j : PB * (j + 1)
            ]
    turn = lax.broadcasted_iota(jnp.int32, (blocks, PB), 1).astype(F32)
    mark = upright(local) + 1.0
    count = upright(cell_ref[1:2, :].astype(F32))
    packed[:, 7 * PB : 8 * PB] = jnp.where(turn < count, mark, -mark)
    by_slot = sum(
        jnp.dot(taken, part, preferred_element_type=F32) for part in thirds(packed[...])
    )
    drops_out[...] = by_slot.reshape(n_inner, CAP, WIDE)

    pl.semaphore_wait(barrier, n_inner - 1 + len(region_peers))

    def exchange(src, dst, sems):
        def send(peer):
            pltpu.make_async_remote_copy(
                src_ref=src.at[peer], dst_ref=dst.at[me],
                send_sem=sems.at[0], recv_sem=sems.at[1],
                device_id=(my_region, peer), device_id_type=MESH,
            ).start()

        each_peer(send)
        dst[me] = src[me]

    def whole(src, dst, sems):
        part = pl.ds(0, n_inner - 1)
        return pltpu.make_async_remote_copy(
            src_ref=src.at[part], dst_ref=dst.at[part],
            send_sem=sems.at[0], recv_sem=sems.at[1],
            device_id=(my_region, inner_high), device_id_type=MESH,
        )

    exchange(drops_out, drops_in, out_sems)
    for load in loads[3:]:
        load.wait()

    for x in range(3):
        for f in range(6):
            part = (density_ref, momentum_ref, momentum_ref, momentum_ref, fuel_ref, energy_ref)[f]
            natural[9 * f + 3 * x : 9 * f + 3 * x + 3, :] = (
                part[f - 1, x] if 1 <= f <= 3 else part[x]
            )
    length = 3 * elements
    node_z = lax.broadcasted_iota(jnp.int32, (length, LANES), 0)
    pick_lane = lax.broadcasted_iota(jnp.int32, (length, LANES), 1)
    first_node = 3 * element_of(pick_lane, elements)
    for c in range(3):
        chosen = (node_z == first_node + c).astype(F32)
        pick[:, LANES * c : LANES * (c + 1)] = chosen.astype(BF16)
    for_lanes = sum(
        jnp.dot(part, pick[...], preferred_element_type=F32) for part in thirds(natural[...])
    )
    for c in range(3):
        for f in range(6):
            rows = for_lanes[9 * f : 9 * f + 9, LANES * c : LANES * (c + 1)]
            fields_ref[NODES * f + 9 * c : NODES * f + 9 * c + 9, :] = rows
            if c == 0:
                fields_ref[NODES * f + 27 : NODES * (f + 1), :] = rows[0 : NODES - 27]

    node = lax.broadcasted_iota(jnp.int32, (6 * NODES, LANES), 0) % NODES

    def halo_copies(section, src):
        copies = [
            (src, high_in.at[section, 1], 0, (my_region, inner_low)),
            (src, low_in.at[section, 1], 1, (my_region, inner_high)),
            (src, high_in.at[section, 0], 2, (region_low, me)),
        ]
        if n_region != 2:
            copies.append((src, low_in.at[section, 0], 3, (region_high, me)))
        return [
            pltpu.make_async_remote_copy(
                src_ref=a, dst_ref=b, send_sem=halo_send.at[section, i],
                recv_sem=halo_recv.at[section, i], device_id=dev, device_id_type=MESH,
            )
            for a, b, i, dev in copies
        ]

    def lifts(value, parts, low, high, d):
        stride = STRIDES[d]
        place = node // stride % 3
        first, last = (place == 0) & (node < 27), (place == 2) & (node < 27)
        rows = 6 * NODES
        beyond = jnp.where(
            first, pltpu.roll(low, rows - 2 * stride, 0),
            jnp.where(last, pltpu.roll(high, 2 * stride, 0), value),
        )
        other = flux_parts(beyond)
        wave = 1.5 * jnp.maximum(
            jnp.abs(parts[0][d]) + parts[2], jnp.abs(other[0][d]) + other[2]
        )
        sign = jnp.where(first, 1.5, -1.5)[0:NODES]
        here, there = flux_rows(value, parts, d), flux_rows(beyond, other, d)
        return [
            sign * (there[f] - here[f]) + wave * (field(beyond, f) - field(value, f))
            for f in range(6)
        ]

    def local_fluid(value, parts):
        for d in range(3):
            for f, part in enumerate(flux_rows(value, parts, d)):
                flux_scr[NODES * d : NODES * (d + 1), LANES * f : LANES * (f + 1)] = part
        volume = jnp.dot(
            deriv_ref[...].astype(BF16), jnp.concatenate(halves(flux_scr[...]), 0),
            preferred_element_type=F32,
        )
        along = lifts(value, parts, pltpu.roll(value, 1, 1), pltpu.roll(value, LANES - 1, 1), 2)
        for f in range(6):
            tend[NODES * f : NODES * (f + 1), :] = (
                volume[:, LANES * f : LANES * (f + 1)] + along[f]
            )

    def face_fluid(section, value, parts, halos):
        for copy in halos:
            copy.wait_recv()
        low_x = high_in[section, 0] if n_region == 2 else low_in[section, 0]
        along_x = lifts(value, parts, low_x, high_in[section, 0], 0)
        along_y = lifts(value, parts, low_in[section, 1], high_in[section, 1], 1)
        for f in range(6):
            tend[NODES * f : NODES * (f + 1), :] += along_x[f] + along_y[f]

    halos_one = halo_copies(0, fields_ref)
    for copy in halos_one:
        copy.start()
    value = fields_ref[...]
    parts = flux_parts(value)
    local_fluid(value, parts)
    face_fluid(0, value, parts, halos_one)
    deposits[...] = jnp.zeros_like(deposits)

    whole(drops_out, drops_in, out_sems).wait_recv()
    arrived = drops_in[...].reshape(slots, WIDE).T
    pos = [arrived[PB * q : PB * (q + 1)] for q in range(3)]
    vel = [arrived[PB * (3 + q) : PB * (4 + q)] for q in range(3)]
    mark = arrived[7 * PB : 8 * PB]
    live = jnp.where(mark > 0.0, 1.0, 0.0)
    mass = jnp.where(mark == 0.0, 1.0, arrived[6 * PB : 7 * PB])
    place = jnp.maximum(jnp.abs(mark[0:1]) - 1.0, 0.0)
    hot_lane = lax.broadcasted_iota(jnp.int32, (LANES, slots), 0).astype(F32)
    hot = element_of(hot_lane, elements) == place
    hot = hot.astype(F32).astype(BF16)
    basis = [(0.5 * t * (t - 1.0), 1.0 - t * t, 0.5 * t * (t + 1.0)) for t in pos]
    for c in range(3):
        for a in range(3):
            pair = basis[0][a] * basis[2][c]
            for b in range(3):
                at = PB * (9 * c + 3 * a + b)
                weights[at : at + PB, :] = pair * basis[1][b]
    lane = lax.broadcasted_iota(jnp.int32, (SENT, LANES), 1)

    def drop_section(value, vel, mass):
        held = jnp.where(lane < elements, value[0:SENT], 0.0)
        gathered[...] = sum(
            jnp.dot(part, hot, preferred_element_type=F32) for part in thirds(held)
        )
        gas = [0.0] * 5
        for k in range(27):
            w = weights[PB * k : PB * (k + 1), :]
            for f in range(5):
                gas[f] = gas[f] + gathered[NODES * f + k : NODES * f + k + 1, :] * w
        inverse = 1.0 / gas[0]
        rel = [gas[1 + c] * inverse - vel[c] for c in range(3)]
        cube_root = jnp.exp(jnp.log(mass) * (1.0 / 3.0))
        drag = live / (cube_root * cube_root)
        accel = [drag * rel[c] for c in range(3)]
        evap = (
            live * EVAP_RATE * cube_root
            * jnp.sqrt(1.0 + (rel[0] * rel[0] + rel[1] * rel[1] + rel[2] * rel[2]))
            * (1.0 - gas[4] * inverse)
        )
        force = [mass * accel[c] for c in range(3)]
        work = sum(force[c] * vel[c] for c in range(3))
        speed_two = sum(vel[c] * vel[c] for c in range(3))
        sources = [evap] + [evap * vel[c] - force[c] for c in range(3)]
        sources.append(evap * (LATENT + 0.5 * speed_two) - work)
        return accel, evap, sources

    def deposit(sources):
        for k in range(27):
            w = weights[PB * k : PB * (k + 1), :]
            for f in range(5):
                deposits[NODES * f + k : NODES * f + k + 1, :] = jnp.sum(
                    w * sources[f], 0, keepdims=True
                )
        summed = sum(nt_dot(part, hot) for part in halves(deposits[...]))
        scale = scale_ref[...] * parcel
        return [scale * field(summed, source) for source in (0, 1, 2, 3, 0, 4)]

    accel, evap, sources = drop_section(value, vel, mass)
    added = deposit(sources)
    for f in range(6):
        rows = slice(NODES * f, NODES * (f + 1))
        fields_one[rows, :] = field(value, f) + TIME_STEP * (tend[rows, :] + added[f])
    halos_two = halo_copies(1, fields_one)
    for copy in halos_two:
        copy.start()
    vel_one = [vel[c] + TIME_STEP * accel[c] for c in range(3)]
    mass_one = mass - TIME_STEP * evap
    value = fields_one[...]
    accel, evap, sources = drop_section(value, vel_one, mass_one)
    final = [0.5 * vel[c] + 0.5 * (vel_one[c] + TIME_STEP * accel[c]) for c in range(3)]
    final.append(0.5 * mass + 0.5 * (mass_one - TIME_STEP * evap))
    back_out[...] = jnp.concatenate(final, 0).T.reshape(n_inner, CAP, LANES)
    exchange(back_out, back_in, back_sems)

    parts = flux_parts(value)
    local_fluid(value, parts)
    added = deposit(sources)
    face_fluid(1, value, parts, halos_two)
    own_lane = lax.broadcasted_iota(jnp.int32, (NODES, LANES), 1) < elements
    for f in range(6):
        rows = slice(NODES * f, NODES * (f + 1))
        ended = 0.5 * fields_ref[rows, :] + 0.5 * (
            field(value, f) + TIME_STEP * (tend[rows, :] + added[f])
        )
        ended = jnp.where(own_lane, ended, 0.0)
        for c in range(3):
            by_lane[9 * f : 9 * f + 9, LANES * c : LANES * (c + 1)] = ended[9 * c : 9 * c + 9]
    grid = sum(nt_dot(part, pick[...]) for part in thirds(by_lane[...]))
    for f, target in enumerate((0, 1, 2, 3, 5, 4)):
        for x in range(3):
            gas_out[target, x] = grid[9 * f + 3 * x : 9 * f + 3 * x + 3]

    whole(back_out, back_in, back_sems).wait_recv()
    came = back_in[...].reshape(slots, LANES)
    by_block = sum(jnp.dot(taken_up, part, preferred_element_type=F32) for part in thirds(came))
    for q in range(4):
        for j in range(PER_LINE):
            placed_out[q, :, PB * j : PB * (j + 1)] = by_block[
                lines_n * j : lines_n * (j + 1), PB * q : PB * (q + 1)
            ]
    for q in range(4):
        for r in range(lines_n):
            dst = mass_out if q == 3 else vel_out
            dst[q % 3 : q % 3 + 1, LANES * r : LANES * (r + 1)] = placed_out[q, r : r + 1, :]

    whole(drops_out, drops_in, out_sems).wait_send()
    whole(back_out, back_in, back_sems).wait_send()
    for copy in halos_one + halos_two:
        copy.wait_send()


def lane_split(elements):
    assert elements <= LANES <= 3 * elements
    return (LANES - elements) // 2


def element_of(lane_id, elements):
    extra = lane_split(elements)
    return jnp.where(
        lane_id < elements, lane_id,
        jnp.where(lane_id < elements + extra, lane_id - elements, lane_id - (LANES - elements)),
    )


def on_device(
    density, momentum, energy, fuel_density, drop_pos, drop_vel, drop_mass, block_cell, block_count
):
    n_inner = lax.axis_size("inner")
    elements = density.shape[2] // 3
    blocks = block_cell.shape[0]
    drops = blocks * PB
    slots = n_inner * CAP
    parcel = 4.0 * elements / drops

    cells = jnp.stack([block_cell, block_count]).reshape(2, blocks // PER_LINE, PER_LINE)
    cells = cells.transpose(0, 2, 1).reshape(2, blocks)

    vmem = pl.BlockSpec(memory_space=pltpu.VMEM)
    hbm = pl.BlockSpec(memory_space=pltpu.HBM)
    loaded = (
        density, momentum, energy, fuel_density, drop_pos, drop_vel, drop_mass.reshape(1, drops),
        jnp.asarray(derivative_rows()), jnp.asarray(node_scale()),
    )
    lines_n = blocks // PER_LINE
    gas, vel, mass = pl.pallas_call(
        functools.partial(gas_kernel, elements, parcel),
        out_shape=(
            jax.ShapeDtypeStruct((6, 3, 3, 3 * elements), F32),
            jax.ShapeDtypeStruct((3, drops), F32),
            jax.ShapeDtypeStruct((1, drops), F32),
        ),
        in_specs=[hbm] * len(loaded) + [vmem],
        out_specs=(vmem, vmem, vmem),
        scratch_shapes=[pltpu.VMEM(x.shape, F32) for x in loaded] + [
            pltpu.VMEM((54, 3 * elements), F32),
            pltpu.VMEM((6 * NODES, LANES), F32),
            pltpu.VMEM((3 * elements, 3 * LANES), BF16),
            pltpu.VMEM((6 * NODES, LANES), F32),
            pltpu.VMEM((6 * NODES, LANES), F32),
            pltpu.VMEM((3 * NODES, 6 * LANES), F32),
            pltpu.VMEM((7, lines_n, LANES), F32),
            pltpu.VMEM((blocks, WIDE), F32),
            pltpu.VMEM((27 * PB, slots), F32),
            pltpu.VMEM((SENT, slots), F32),
            pltpu.VMEM((SENT, slots), F32),
            pltpu.VMEM((n_inner, CAP, WIDE), F32),
            pltpu.VMEM((n_inner, CAP, WIDE), F32),
            pltpu.VMEM((n_inner, CAP, LANES), F32),
            pltpu.VMEM((n_inner, CAP, LANES), F32),
            pltpu.VMEM((2, 2, 6 * NODES, LANES), F32),
            pltpu.VMEM((2, 2, 6 * NODES, LANES), F32),
            pltpu.VMEM((54, 3 * LANES), F32),
            pltpu.VMEM((4, lines_n, LANES), F32),
            pltpu.SemaphoreType.DMA((len(loaded),)),
            pltpu.SemaphoreType.DMA((2,)),
            pltpu.SemaphoreType.DMA((2,)),
            pltpu.SemaphoreType.DMA((2, 4)),
            pltpu.SemaphoreType.DMA((2, 4)),
        ],
        compiler_params=pltpu.CompilerParams(
            collective_id=0, has_side_effects=True, vmem_limit_bytes=62 * 1024 * 1024
        ),
    )(*loaded, cells)
    return gas, vel, mass.reshape(drops)


def solution(mesh):
    placed = (
        P("region", "inner", None),
        P(None, "region", "inner", None),
        P("region", "inner", None),
        P("region", "inner", None),
        P(None, ("region", "inner")),
        P(None, ("region", "inner")),
        P(("region", "inner")),
        P(("region", "inner")),
        P(("region", "inner")),
    )
    return jax.shard_map(
        on_device,
        mesh=mesh,
        in_specs=placed,
        out_specs=(
            P(None, "region", "inner", None),
            P(None, ("region", "inner")),
            P(("region", "inner")),
        ),
        check_vma=False,
    )
```

```python
import functools

import jax
import jax.numpy as jnp
import numpy as np
from jax import lax
from jax.experimental import pallas as pl
from jax.experimental.pallas import tpu as pltpu
from jax.sharding import PartitionSpec as P

PB = 32
CAP = 8
GAMMA = 1.4
TIME_STEP = 0.05
EVAP_RATE = 0.5
LATENT = 0.5
LANES = 128
PER_LINE = LANES // PB
NODES = 32
SENT = 5 * NODES
WIDE = 256
STRIDES = (3, 1, 9)
F32, BF16 = jnp.float32, jnp.bfloat16
MESH = pl.DeviceIdType.MESH


def derivative_rows():
    line = np.array([[-1.5, 2.0, -0.5], [-0.5, 0.0, 0.5], [0.5, -2.0, 1.5]])
    table = np.zeros((NODES, 3 * NODES))
    for node in range(27):
        for d, stride in enumerate(STRIDES):
            place = node // stride % 3
            for j in range(3):
                table[node, d * NODES + node + (j - place) * stride] = -line[place, j]
    return np.concatenate([table, table], 1).astype(np.float32)


def node_scale():
    q = np.array([1.0 / 3.0, 4.0 / 3.0, 1.0 / 3.0])
    table = np.zeros((NODES, LANES), np.float32)
    for node in range(27):
        table[node] = 1.0 / (q[node // 3 % 3] * q[node % 3] * q[node // 9])
    return table


def halves(value):
    high = value.astype(BF16)
    return high, (value - high.astype(F32)).astype(BF16)


def thirds(value):
    high = value.astype(BF16)
    rest = value - high.astype(F32)
    return (high,) + halves(rest)


def nt_dot(left, right):
    return lax.dot_general(left, right, (((1,), (1,)), ((), ())), preferred_element_type=F32)


def field(value, f):
    return value[NODES * f : NODES * (f + 1)]


def flux_parts(value):
    inverse = 1.0 / field(value, 0)
    speeds = [field(value, 1 + c) * inverse for c in range(3)]
    kinetic = sum(field(value, 1 + c) * speeds[c] for c in range(3))
    pressure = (GAMMA - 1.0) * (field(value, 5) - 0.5 * kinetic)
    sound = jnp.sqrt(GAMMA * pressure * inverse)
    return speeds, pressure, sound


def flux_rows(value, parts, d):
    speeds, pressure, _ = parts
    speed = speeds[d]
    rows = [field(value, 1 + d)]
    for c in range(3):
        row = field(value, 1 + c) * speed
        rows.append(row + pressure if c == d else row)
    rows.append(field(value, 4) * speed)
    rows.append((field(value, 5) + pressure) * speed)
    return rows


def gas_kernel(
    elements, parcel,
    density_hbm, momentum_hbm, energy_hbm, fuel_hbm, pos_hbm, vel_hbm, mass_hbm, deriv_hbm,
    scale_hbm, cell_hbm, count_hbm,
    gas_out, vel_out, mass_out,
    density_ref, momentum_ref, energy_ref, fuel_ref, pos_ref, vel_ref, mass_ref, deriv_ref,
    scale_ref, cell_ref, count_ref,
    natural, fields_ref, pick, fields_one, tend, flux_scr, lines, packed, weights, gathered,
    deposits, drops_out, drops_in, back_out, back_in, low_in, high_in, by_lane, placed_out,
    in_sems, out_sems, back_sems, halo_send, halo_recv,
):
    n_inner, n_region = lax.axis_size("inner"), lax.axis_size("region")
    me, my_region = lax.axis_index("inner"), lax.axis_index("region")
    slots = n_inner * CAP
    blocks = cell_ref.shape[1]
    lines_n = blocks // PER_LINE
    inner_low, inner_high = lax.rem(me + n_inner - 1, n_inner), lax.rem(me + 1, n_inner)
    region_low = lax.rem(my_region + n_region - 1, n_region)
    region_high = lax.rem(my_region + 1, n_region)

    loads = [
        pltpu.make_async_copy(src, dst, in_sems.at[n])
        for n, (src, dst) in enumerate((
            (pos_hbm, pos_ref), (vel_hbm, vel_ref), (mass_hbm, mass_ref),
            (density_hbm, density_ref), (momentum_hbm, momentum_ref), (energy_hbm, energy_ref),
            (fuel_hbm, fuel_ref), (deriv_hbm, deriv_ref), (scale_hbm, scale_ref),
            (cell_hbm, cell_ref), (count_hbm, count_ref),
        ))
    ]
    for load in loads[9:] + loads[:9]:
        load.start()

    bits = [1 << n for n in range((n_inner - 1).bit_length())]
    paired = n_inner == 1 << len(bits)

    def peer_of(j):
        if not paired:
            return lax.rem(me + j, n_inner)
        return sum((me // b % 2 + j // b % 2) % 2 * b for b in bits)

    def each_peer(body):
        if n_inner <= 16:
            for j in range(n_inner - 1, 0, -1):
                body(peer_of(j))
        else:
            @pl.loop(1, n_inner)
            def _(j):
                body(peer_of(n_inner - j))

    barrier = pltpu.get_barrier_semaphore()

    def greet(peer):
        pl.semaphore_signal(barrier, inc=1, device_id=(my_region, peer), device_id_type=MESH)

    each_peer(greet)
    region_peers = [region_high] if n_region == 2 else [region_low, region_high]
    for other in region_peers:
        pl.semaphore_signal(barrier, inc=1, device_id=(other, me), device_id_type=MESH)

    for load in loads[9:]:
        load.wait()
    lane_b = lax.broadcasted_iota(jnp.int32, (blocks, blocks), 1)
    block_at = lane_b % lines_n * PER_LINE + lane_b // lines_n
    moved = block_at == lax.broadcasted_iota(jnp.int32, (blocks, blocks), 0)
    moved = moved.astype(F32).astype(BF16)
    both = lax.broadcasted_iota(jnp.int32, (16, blocks), 0) == 0
    both = jnp.where(both, cell_ref[...], count_ref[...]).astype(F32)
    both = sum(jnp.dot(part, moved, preferred_element_type=F32) for part in halves(both))
    cell = both[0:1]
    owner = jnp.floor((cell + 0.5) * (1.0 / elements))
    local = cell - owner * elements
    square = (blocks, blocks)
    diagonal = lax.broadcasted_iota(jnp.int32, square, 0) == lax.broadcasted_iota(
        jnp.int32, square, 1
    )

    def upright(row):
        return jnp.sum(
            jnp.where(diagonal, jnp.broadcast_to(row, square), 0.0), 1, keepdims=True
        )

    down = upright(owner)
    earlier = jnp.sum(jnp.where(down < jnp.broadcast_to(owner, square), 1.0, 0.0), 0, keepdims=True)
    lane_b = lax.broadcasted_iota(jnp.int32, (1, blocks), 1)
    number = (lane_b % lines_n * PER_LINE + lane_b // lines_n).astype(F32)
    slot = owner * CAP + number - earlier
    taken = lax.broadcasted_iota(jnp.int32, (slots, blocks), 0).astype(F32) == slot
    taken = taken.astype(F32).astype(BF16)
    taken_up = lax.broadcasted_iota(jnp.int32, (blocks, slots), 1).astype(F32) == upright(slot)
    taken_up = taken_up.astype(F32).astype(BF16)

    for load in loads[:3]:
        load.wait()
    for q in range(7):
        src = (pos_ref, vel_ref, mass_ref)[q // 3]
        for r in range(lines_n):
            lines[q, r : r + 1, :] = src[q % 3 : q % 3 + 1, LANES * r : LANES * (r + 1)]
    for q in range(7):
        for j in range(PER_LINE):
            packed[lines_n * j : lines_n * (j + 1), PB * q : PB * (q + 1)] = lines[
                q, :, PB * j : PB * (j + 1)
            ]
    turn = lax.broadcasted_iota(jnp.int32, (blocks, PB), 1).astype(F32)
    mark = upright(local) + 1.0
    count = upright(both[1:2])
    packed[:, 7 * PB : 8 * PB] = jnp.where(turn < count, mark, -mark)
    by_slot = sum(
        jnp.dot(taken, part, preferred_element_type=F32) for part in thirds(packed[...])
    )
    drops_out[...] = by_slot.reshape(n_inner, CAP, WIDE)

    pl.semaphore_wait(barrier, n_inner - 1 + len(region_peers))

    def exchange(src, dst, sems):
        def send(peer):
            pltpu.make_async_remote_copy(
                src_ref=src.at[peer], dst_ref=dst.at[me],
                send_sem=sems.at[0], recv_sem=sems.at[1],
                device_id=(my_region, peer), device_id_type=MESH,
            ).start()

        each_peer(send)
        dst[me] = src[me]

    def whole(src, dst, sems):
        part = pl.ds(0, n_inner - 1)
        return pltpu.make_async_remote_copy(
            src_ref=src.at[part], dst_ref=dst.at[part],
            send_sem=sems.at[0], recv_sem=sems.at[1],
            device_id=(my_region, inner_high), device_id_type=MESH,
        )

    exchange(drops_out, drops_in, out_sems)
    for load in loads[3:9]:
        load.wait()

    for x in range(3):
        for f in range(6):
            part = (density_ref, momentum_ref, momentum_ref, momentum_ref, fuel_ref, energy_ref)[f]
            natural[9 * f + 3 * x : 9 * f + 3 * x + 3, :] = (
                part[f - 1, x] if 1 <= f <= 3 else part[x]
            )
    length = 3 * elements
    node_z = lax.broadcasted_iota(jnp.int32, (length, LANES), 0)
    pick_lane = lax.broadcasted_iota(jnp.int32, (length, LANES), 1)
    first_node = 3 * element_of(pick_lane, elements)
    for c in range(3):
        chosen = (node_z == first_node + c).astype(F32)
        pick[:, LANES * c : LANES * (c + 1)] = chosen.astype(BF16)
    for_lanes = sum(
        jnp.dot(part, pick[...], preferred_element_type=F32) for part in thirds(natural[...])
    )
    for c in range(3):
        for f in range(6):
            rows = for_lanes[9 * f : 9 * f + 9, LANES * c : LANES * (c + 1)]
            fields_ref[NODES * f + 9 * c : NODES * f + 9 * c + 9, :] = rows
            if c == 0:
                fields_ref[NODES * f + 27 : NODES * (f + 1), :] = rows[0 : NODES - 27]

    node = lax.broadcasted_iota(jnp.int32, (6 * NODES, LANES), 0) % NODES

    def halo_copies(section, src):
        copies = [
            (src, high_in.at[section, 1], 0, (my_region, inner_low)),
            (src, low_in.at[section, 1], 1, (my_region, inner_high)),
            (src, high_in.at[section, 0], 2, (region_low, me)),
        ]
        if n_region != 2:
            copies.append((src, low_in.at[section, 0], 3, (region_high, me)))
        return [
            pltpu.make_async_remote_copy(
                src_ref=a, dst_ref=b, send_sem=halo_send.at[section, i],
                recv_sem=halo_recv.at[section, i], device_id=dev, device_id_type=MESH,
            )
            for a, b, i, dev in copies
        ]

    def lifts(value, parts, low, high, d):
        stride = STRIDES[d]
        place = node // stride % 3
        first, last = (place == 0) & (node < 27), (place == 2) & (node < 27)
        rows = 6 * NODES
        beyond = jnp.where(
            first, pltpu.roll(low, rows - 2 * stride, 0),
            jnp.where(last, pltpu.roll(high, 2 * stride, 0), value),
        )
        other = flux_parts(beyond)
        wave = 1.5 * jnp.maximum(
            jnp.abs(parts[0][d]) + parts[2], jnp.abs(other[0][d]) + other[2]
        )
        sign = jnp.where(first, 1.5, -1.5)[0:NODES]
        here, there = flux_rows(value, parts, d), flux_rows(beyond, other, d)
        return [
            sign * (there[f] - here[f]) + wave * (field(beyond, f) - field(value, f))
            for f in range(6)
        ]

    def local_fluid(value, parts):
        for d in range(3):
            for f, part in enumerate(flux_rows(value, parts, d)):
                flux_scr[NODES * d : NODES * (d + 1), LANES * f : LANES * (f + 1)] = part
        volume = jnp.dot(
            deriv_ref[...].astype(BF16), jnp.concatenate(halves(flux_scr[...]), 0),
            preferred_element_type=F32,
        )
        along = lifts(value, parts, pltpu.roll(value, 1, 1), pltpu.roll(value, LANES - 1, 1), 2)
        for f in range(6):
            tend[NODES * f : NODES * (f + 1), :] = (
                volume[:, LANES * f : LANES * (f + 1)] + along[f]
            )

    def face_fluid(section, value, parts, halos):
        for copy in halos:
            copy.wait_recv()
        low_x = high_in[section, 0] if n_region == 2 else low_in[section, 0]
        along_x = lifts(value, parts, low_x, high_in[section, 0], 0)
        along_y = lifts(value, parts, low_in[section, 1], high_in[section, 1], 1)
        for f in range(6):
            tend[NODES * f : NODES * (f + 1), :] += along_x[f] + along_y[f]

    halos_one = halo_copies(0, fields_ref)
    for copy in halos_one:
        copy.start()
    value = fields_ref[...]
    parts = flux_parts(value)
    local_fluid(value, parts)
    face_fluid(0, value, parts, halos_one)
    deposits[...] = jnp.zeros_like(deposits)

    whole(drops_out, drops_in, out_sems).wait_recv()
    arrived = drops_in[...].reshape(slots, WIDE).T
    pos = [arrived[PB * q : PB * (q + 1)] for q in range(3)]
    vel = [arrived[PB * (3 + q) : PB * (4 + q)] for q in range(3)]
    mark = arrived[7 * PB : 8 * PB]
    live = jnp.where(mark > 0.0, 1.0, 0.0)
    mass = jnp.where(mark == 0.0, 1.0, arrived[6 * PB : 7 * PB])
    place = jnp.maximum(jnp.abs(mark[0:1]) - 1.0, 0.0)
    hot_lane = lax.broadcasted_iota(jnp.int32, (LANES, slots), 0).astype(F32)
    hot = element_of(hot_lane, elements) == place
    hot = hot.astype(F32).astype(BF16)
    basis = [(0.5 * t * (t - 1.0), 1.0 - t * t, 0.5 * t * (t + 1.0)) for t in pos]
    for c in range(3):
        for a in range(3):
            pair = basis[0][a] * basis[2][c]
            for b in range(3):
                at = PB * (9 * c + 3 * a + b)
                weights[at : at + PB, :] = pair * basis[1][b]
    lane = lax.broadcasted_iota(jnp.int32, (SENT, LANES), 1)

    def drop_section(value, vel, mass):
        held = jnp.where(lane < elements, value[0:SENT], 0.0)
        gathered[...] = sum(
            jnp.dot(part, hot, preferred_element_type=F32) for part in thirds(held)
        )
        gas = [0.0] * 5
        for k in range(27):
            w = weights[PB * k : PB * (k + 1), :]
            for f in range(5):
                gas[f] = gas[f] + gathered[NODES * f + k : NODES * f + k + 1, :] * w
        inverse = 1.0 / gas[0]
        rel = [gas[1 + c] * inverse - vel[c] for c in range(3)]
        cube_root = jnp.exp(jnp.log(mass) * (1.0 / 3.0))
        drag = live / (cube_root * cube_root)
        accel = [drag * rel[c] for c in range(3)]
        evap = (
            live * EVAP_RATE * cube_root
            * jnp.sqrt(1.0 + (rel[0] * rel[0] + rel[1] * rel[1] + rel[2] * rel[2]))
            * (1.0 - gas[4] * inverse)
        )
        force = [mass * accel[c] for c in range(3)]
        work = sum(force[c] * vel[c] for c in range(3))
        speed_two = sum(vel[c] * vel[c] for c in range(3))
        sources = [evap] + [evap * vel[c] - force[c] for c in range(3)]
        sources.append(evap * (LATENT + 0.5 * speed_two) - work)
        return accel, evap, sources

    def deposit(sources):
        for k in range(27):
            w = weights[PB * k : PB * (k + 1), :]
            for f in range(5):
                deposits[NODES * f + k : NODES * f + k + 1, :] = jnp.sum(
                    w * sources[f], 0, keepdims=True
                )
        summed = sum(nt_dot(part, hot) for part in halves(deposits[...]))
        scale = scale_ref[...] * parcel
        return [scale * field(summed, source) for source in (0, 1, 2, 3, 0, 4)]

    accel, evap, sources = drop_section(value, vel, mass)
    added = deposit(sources)
    for f in range(6):
        rows = slice(NODES * f, NODES * (f + 1))
        fields_one[rows, :] = field(value, f) + TIME_STEP * (tend[rows, :] + added[f])
    halos_two = halo_copies(1, fields_one)
    for copy in halos_two:
        copy.start()
    vel_one = [vel[c] + TIME_STEP * accel[c] for c in range(3)]
    mass_one = mass - TIME_STEP * evap
    value = fields_one[...]
    accel, evap, sources = drop_section(value, vel_one, mass_one)
    final = [0.5 * vel[c] + 0.5 * (vel_one[c] + TIME_STEP * accel[c]) for c in range(3)]
    final.append(0.5 * mass + 0.5 * (mass_one - TIME_STEP * evap))
    back_out[...] = jnp.concatenate(final, 0).T.reshape(n_inner, CAP, LANES)
    exchange(back_out, back_in, back_sems)

    parts = flux_parts(value)
    local_fluid(value, parts)
    added = deposit(sources)
    face_fluid(1, value, parts, halos_two)
    own_lane = lax.broadcasted_iota(jnp.int32, (NODES, LANES), 1) < elements
    for f in range(6):
        rows = slice(NODES * f, NODES * (f + 1))
        ended = 0.5 * fields_ref[rows, :] + 0.5 * (
            field(value, f) + TIME_STEP * (tend[rows, :] + added[f])
        )
        ended = jnp.where(own_lane, ended, 0.0)
        for c in range(3):
            by_lane[9 * f : 9 * f + 9, LANES * c : LANES * (c + 1)] = ended[9 * c : 9 * c + 9]
    grid = sum(nt_dot(part, pick[...]) for part in thirds(by_lane[...]))
    for f, target in enumerate((0, 1, 2, 3, 5, 4)):
        for x in range(3):
            gas_out[target, x] = grid[9 * f + 3 * x : 9 * f + 3 * x + 3]

    whole(back_out, back_in, back_sems).wait_recv()
    came = back_in[...].reshape(slots, LANES)
    by_block = sum(jnp.dot(taken_up, part, preferred_element_type=F32) for part in thirds(came))
    for q in range(4):
        for j in range(PER_LINE):
            placed_out[q, :, PB * j : PB * (j + 1)] = by_block[
                lines_n * j : lines_n * (j + 1), PB * q : PB * (q + 1)
            ]
    for q in range(4):
        for r in range(lines_n):
            dst = mass_out if q == 3 else vel_out
            dst[q % 3 : q % 3 + 1, LANES * r : LANES * (r + 1)] = placed_out[q, r : r + 1, :]

    whole(drops_out, drops_in, out_sems).wait_send()
    whole(back_out, back_in, back_sems).wait_send()
    for copy in halos_one + halos_two:
        copy.wait_send()


def lane_split(elements):
    assert elements <= LANES <= 3 * elements
    return (LANES - elements) // 2


def element_of(lane_id, elements):
    extra = lane_split(elements)
    return jnp.where(
        lane_id < elements, lane_id,
        jnp.where(lane_id < elements + extra, lane_id - elements, lane_id - (LANES - elements)),
    )


def on_device(
    density, momentum, energy, fuel_density, drop_pos, drop_vel, drop_mass, block_cell, block_count
):
    n_inner = lax.axis_size("inner")
    elements = density.shape[2] // 3
    blocks = block_cell.shape[0]
    drops = blocks * PB
    slots = n_inner * CAP
    parcel = 4.0 * elements / drops

    vmem = pl.BlockSpec(memory_space=pltpu.VMEM)
    hbm = pl.BlockSpec(memory_space=pltpu.HBM)
    loaded = (
        density, momentum, energy, fuel_density, drop_pos, drop_vel, drop_mass.reshape(1, drops),
        jnp.asarray(derivative_rows()), jnp.asarray(node_scale()),
        block_cell.reshape(1, blocks), block_count.reshape(1, blocks),
    )
    lines_n = blocks // PER_LINE
    gas, vel, mass = pl.pallas_call(
        functools.partial(gas_kernel, elements, parcel),
        out_shape=(
            jax.ShapeDtypeStruct((6, 3, 3, 3 * elements), F32),
            jax.ShapeDtypeStruct((3, drops), F32),
            jax.ShapeDtypeStruct((1, drops), F32),
        ),
        in_specs=[hbm] * len(loaded),
        out_specs=(vmem, vmem, vmem),
        scratch_shapes=[pltpu.VMEM(x.shape, x.dtype) for x in loaded] + [
            pltpu.VMEM((54, 3 * elements), F32),
            pltpu.VMEM((6 * NODES, LANES), F32),
            pltpu.VMEM((3 * elements, 3 * LANES), BF16),
            pltpu.VMEM((6 * NODES, LANES), F32),
            pltpu.VMEM((6 * NODES, LANES), F32),
            pltpu.VMEM((3 * NODES, 6 * LANES), F32),
            pltpu.VMEM((7, lines_n, LANES), F32),
            pltpu.VMEM((blocks, WIDE), F32),
            pltpu.VMEM((27 * PB, slots), F32),
            pltpu.VMEM((SENT, slots), F32),
            pltpu.VMEM((SENT, slots), F32),
            pltpu.VMEM((n_inner, CAP, WIDE), F32),
            pltpu.VMEM((n_inner, CAP, WIDE), F32),
            pltpu.VMEM((n_inner, CAP, LANES), F32),
            pltpu.VMEM((n_inner, CAP, LANES), F32),
            pltpu.VMEM((2, 2, 6 * NODES, LANES), F32),
            pltpu.VMEM((2, 2, 6 * NODES, LANES), F32),
            pltpu.VMEM((54, 3 * LANES), F32),
            pltpu.VMEM((4, lines_n, LANES), F32),
            pltpu.SemaphoreType.DMA((len(loaded),)),
            pltpu.SemaphoreType.DMA((2,)),
            pltpu.SemaphoreType.DMA((2,)),
            pltpu.SemaphoreType.DMA((2, 4)),
            pltpu.SemaphoreType.DMA((2, 4)),
        ],
        compiler_params=pltpu.CompilerParams(
            collective_id=0, has_side_effects=True, vmem_limit_bytes=62 * 1024 * 1024
        ),
    )(*loaded)
    return gas, vel, mass.reshape(drops)


def solution(mesh):
    placed = (
        P("region", "inner", None),
        P(None, "region", "inner", None),
        P("region", "inner", None),
        P("region", "inner", None),
        P(None, ("region", "inner")),
        P(None, ("region", "inner")),
        P(("region", "inner")),
        P(("region", "inner")),
        P(("region", "inner")),
    )
    return jax.shard_map(
        on_device,
        mesh=mesh,
        in_specs=placed,
        out_specs=(
            P(None, "region", "inner", None),
            P(None, ("region", "inner")),
            P(("region", "inner")),
        ),
        check_vma=False,
    )
```
